32 devices in a mesh: ctx: 8 (over z, core), head: 4 (over y, x).
Axes of the slice: x: 2, y: 2, z: 4, core: 2. Of those that a mesh axis runs over, the one named last changes fastest.
Arguments:
- hidden_in: bfloat16 [2048, 8192], P('ctx', 'head'), may hold values from -90 to 90
- query_rows: bfloat16 [2048, 8192], P('ctx', 'head'), may hold values from -5 to 5
- key_rows: bfloat16 [2048, 1024], P('ctx', 'head'), may hold values from -5 to 5
- value_rows: bfloat16 [2048, 1024], P('ctx', 'head'), may hold values from -6 to 6
- out_weight: bfloat16 [8192, 8192], P('head'), may hold values from -0.0625 to 0.0625
- grad_out: bfloat16 [2048, 8192], P('ctx', 'head'), may hold values from -6 to 6
- answer_mask: int32 [2048], P('ctx'), may hold values 0 or 1
Outputs:
- grad_query: bfloat16 [2048, 8192], P('ctx', 'head')
- grad_key: bfloat16 [2048, 1024], P('ctx', 'head')
- grad_value: bfloat16 [2048, 1024], P('ctx', 'head')
- fisher_q: float32 [8, 64], P('ctx', 'head')
- fisher_o: float32 [8, 64], P('ctx', 'head')
The draws below stay inside these ranges and needn't reach their ends.
All inputs are finite; a program needn't handle non-finite values. No bound on the sum of `answer_mask` on one device may be relied on, other than what follows from the above.
Results may differ from the reference program's by a relative error of at most 0.019.
Values may be sent and summed in bfloat16 or wider, within the bound.
A program may use at most 128 MiB of HBM per device.

```python
import jax
import jax.numpy as jnp
from jax import lax

D = 8192
HEADS = 64
KVH = 8
HD = 128
TOK_DEV = 256
TOKENS = 2048


def draw_hidden_in(key, part):
    column = jnp.arange(D, dtype=jnp.float32) / (D - 1)
    factor = jax.random.uniform(jax.random.fold_in(key, 31), (D,), jnp.float32, 0.7, 1.4)
    column_scale = jnp.exp(column * jnp.log(10.0)) * factor
    base = jax.random.truncated_normal(jax.random.fold_in(key, 33), -6.0, 6.0, (TOKENS, D), jnp.float32)
    return (base * column_scale[None, :]).astype(jnp.bfloat16)


def drawn_pair(key):
    width_q = HEADS * HD
    width_k = KVH * HD
    queries = jax.random.truncated_normal(jax.random.fold_in(key, 21), -5.0, 5.0, (TOKENS, width_q), jnp.float32)
    key_table = jax.random.truncated_normal(jax.random.fold_in(key, 22), -5.0, 5.0, (TOKENS, width_k), jnp.float32)
    return (queries, key_table)


def draw_query_rows(key, part):
    return drawn_pair(key)[0].astype(jnp.bfloat16)


def draw_key_rows(key, part):
    return drawn_pair(key)[1].astype(jnp.bfloat16)


def touch_ends(drawn, key, low, top_value):
    extent = drawn.shape
    index_at = [jax.random.randint(jax.random.fold_in(key, axis), (), 0, extent[axis]) for axis in range(len(extent))]
    drawn = drawn.at[tuple(index_at)].set(low)
    longest = extent.index(max(extent))
    index_at[longest] = (index_at[longest] + 1) % extent[longest]
    return drawn.at[tuple(index_at)].set(top_value)


def shard_levels(own_key, extent, shards, low, top_value):
    def one(axis_at, blocks):
        steps = jax.random.uniform(jax.random.fold_in(jax.random.fold_in(own_key, 6), axis_at), (blocks,), jnp.float32, low / len(shards), top_value / len(shards))
        return jnp.repeat(jnp.exp(steps), extent[axis_at] // blocks).reshape((-1,) + (1,) * (len(extent) - axis_at - 1))

    factor_of = one(*shards[0])
    for cut in shards[1:]:
        factor_of = factor_of * one(*cut)
    return factor_of


def noise(stream_key, dims, spread, bound, shards=(), kind=jnp.bfloat16):
    factor_of = shard_levels(stream_key, dims, shards, -0.22, 0.18) if shards else 1.0
    result = jax.random.normal(stream_key, dims, jnp.float32) * spread * factor_of
    return jnp.minimum(jnp.maximum(result, -bound), bound).astype(kind)


def setup_inputs(seed: int = 0) -> dict:
    seeds = jax.random.split(jax.random.key(seed), 8)
    hidden_in = draw_hidden_in(jax.random.fold_in(seeds[7], 71), 0)
    query_rows = draw_query_rows(jax.random.fold_in(seeds[7], 71), 0)
    key_rows = draw_key_rows(jax.random.fold_in(seeds[7], 71), 0)
    value_rows = noise(seeds[3], (TOKENS, KVH * HD), 1.0, 6.0, ((0, 8), (1, 4)))
    out_weight = noise(seeds[4], (HEADS * HD, D), D ** -0.5, 0.0625, ((0, 4),))
    grad_out = noise(seeds[5], (TOKENS, D), 1.0, 6.0, ((0, 8), (1, 4)))
    answer_mask = touch_ends((jax.random.randint(seeds[6], (TOKENS,), 0, 4) < 1).astype(jnp.int32), jax.random.fold_in(seeds[6], 1), 0, 1)
    return {"hidden_in": hidden_in, "query_rows": query_rows, "key_rows": key_rows, "value_rows": value_rows, "out_weight": out_weight, "grad_out": grad_out, "answer_mask": answer_mask}


NEGATIVE = -1e30
EPSILON = 1e-6


def span_fisher(left_side, right_side):
    def span_squares(operands):
        product = jnp.dot(operands[0].T, operands[1], preferred_element_type=jnp.float32)
        return jnp.sum((product * product).reshape(product.shape[0], HEADS, HD), axis=(0, 2))
    squares = lax.map(span_squares, (left_side, right_side))
    return jnp.log(squares / (D * HD * TOK_DEV) + EPSILON)


def reference(hidden_in, query_rows, key_rows, value_rows, out_weight, grad_out, answer_mask):
    tokens = query_rows.shape[0]
    group_size = HEADS // KVH
    scaling = HD ** -0.5
    loss_weight = 0.25 + answer_mask.astype(jnp.float32)
    weighted = (grad_out.astype(jnp.float32) * loss_weight[:, None]).astype(jnp.bfloat16)
    grad_attended = jnp.dot(weighted, out_weight.T, preferred_element_type=jnp.float32).astype(jnp.bfloat16)
    query_heads = query_rows.reshape(tokens, KVH, group_size, HD).transpose(1, 0, 2, 3)
    key_heads = key_rows.reshape(tokens, KVH, HD).transpose(1, 0, 2)
    value_heads = value_rows.reshape(tokens, KVH, HD).transpose(1, 0, 2)
    grad_heads = grad_attended.reshape(tokens, KVH, group_size, HD).transpose(1, 0, 2, 3)
    positions = jnp.arange(tokens, dtype=jnp.int32)
    causal = positions[:, None] >= positions[None, :]

    def one_group(operands):
        query_group = operands[0].astype(jnp.float32)
        key_group = operands[1].astype(jnp.float32)
        value_group = operands[2].astype(jnp.float32)
        grad_group = operands[3].astype(jnp.float32)
        scores = jnp.einsum("tgd,kd->tgk", query_group, key_group) * scaling
        scores = jnp.where(causal[:, None, :], scores, NEGATIVE)
        row_max = jnp.max(scores, axis=-1, keepdims=True)
        log_total = row_max + jnp.log(jnp.sum(jnp.exp(scores - row_max), axis=-1, keepdims=True))
        softmax = jnp.exp(scores - log_total)
        rounded = softmax.astype(jnp.bfloat16)
        attended = jnp.einsum("tgk,kd->tgd", rounded.astype(jnp.float32), value_group).astype(jnp.bfloat16)
        row_dot = jnp.sum(grad_group * attended.astype(jnp.float32), axis=-1, keepdims=True)
        grad_prob = jnp.einsum("tgd,kd->tgk", grad_group, value_group)
        grad_score = (softmax * (grad_prob - row_dot) * scaling).astype(jnp.bfloat16)
        grad_query = jnp.einsum("tgk,kd->tgd", grad_score.astype(jnp.float32), key_group).astype(jnp.bfloat16)
        grad_key = jnp.einsum("tgk,tgd->kd", grad_score.astype(jnp.float32), query_group).astype(jnp.bfloat16)
        grad_value = jnp.einsum("tgk,tgd->kd", rounded.astype(jnp.float32), grad_group).astype(jnp.bfloat16)
        return attended, grad_query, grad_key, grad_value

    attended, grad_query, grad_key, grad_value = lax.map(one_group, (query_heads, key_heads, value_heads, grad_heads))
    attended = attended.transpose(1, 0, 2, 3).reshape(tokens, HEADS * HD)
    grad_query = grad_query.transpose(1, 0, 2, 3).reshape(tokens, HEADS * HD)
    grad_key = grad_key.transpose(1, 0, 2).reshape(tokens, KVH * HD)
    grad_value = grad_value.transpose(1, 0, 2).reshape(tokens, KVH * HD)
    span_count = tokens // TOK_DEV
    fisher_q = span_fisher(hidden_in.reshape(span_count, TOK_DEV, D), grad_query.reshape(span_count, TOK_DEV, HEADS * HD))
    fisher_o = span_fisher(weighted.reshape(span_count, TOK_DEV, D), attended.reshape(span_count, TOK_DEV, HEADS * HD))
    return grad_query, grad_key, grad_value, fisher_q, fisher_o
```

```python
import functools

import jax
import jax.numpy as jnp
from jax import lax
from jax.experimental import pallas as pl
from jax.experimental.pallas import tpu as pltpu
from jax.sharding import PartitionSpec as P

HD = 128
GROUP = 8
NEGATIVE = -1e30
EPSILON = 1e-06
SCALING = HD ** (-0.5)
LOG2E = 1.4426950408889634
SCALE2 = SCALING * LOG2E
VMEM_LIMIT = 56 * 1024 * 1024


def dot(left, right, left_dim, right_dim):
    return lax.dot_general(
        left, right, (((left_dim,), (right_dim,)), ((), ())), preferred_element_type=jnp.float32
    )


def columns(index):
    return pl.ds(pl.multiple_of(index * HD, HD), HD)


def causal_keep(rows):
    key_pos = lax.broadcasted_iota(jnp.int32, (rows, rows), 0)
    query_pos = lax.broadcasted_iota(jnp.int32, (rows, rows), 1)
    return key_pos <= query_pos


def forward_kernel(groups, query_ref, kv_ref, attended_ref, log_ref, sum_ref, max_ref, total_ref):
    rows = query_ref.shape[0]
    own = lax.axis_index("ctx")

    def block(number, diagonal):
        row_at = pl.ds(pl.multiple_of(number * rows, rows), rows)

        def one_group(group, _):
            key_block = kv_ref[row_at, columns(group)]
            value_turned = kv_ref[row_at, columns(groups + group)].T
            for member in range(GROUP):
                head = group * GROUP + member
                scores = dot(key_block, query_ref[:, columns(head)], 1, 1)
                one = pl.ds(head, 1)
                if diagonal:
                    scores = jnp.where(causal_keep(rows), scores, NEGATIVE)
                    new_max = jnp.max(scores, axis=0, keepdims=True)
                else:
                    old_max = max_ref[one, :]
                    new_max = jnp.maximum(old_max, jnp.max(scores, axis=0, keepdims=True))
                weights = jnp.exp2(scores * SCALE2 - new_max * SCALE2)
                weights_sum = jnp.sum(weights, axis=0, keepdims=True)
                part = dot(value_turned, weights.astype(jnp.bfloat16), 1, 0)
                if diagonal:
                    total_ref[one, :] = weights_sum
                    sum_ref[columns(head), :] = part
                else:
                    factor = jnp.exp2((old_max - new_max) * SCALE2)
                    total_ref[one, :] = total_ref[one, :] * factor + weights_sum
                    sum_ref[columns(head), :] = sum_ref[columns(head), :] * factor + part
                max_ref[one, :] = new_max
            return 0

        lax.fori_loop(0, groups, one_group, 0)

    block(own, True)

    def step(number, _):
        block(number, False)
        return 0

    lax.fori_loop(0, own, step, 0)
    for head in range(groups * GROUP):
        total = total_ref[head : head + 1, :]
        log_ref[head : head + 1, :] = max_ref[head : head + 1, :] * SCALE2 + jnp.log2(total)
        part = sum_ref[head * HD : (head + 1) * HD, :]
        attended_ref[head * HD : (head + 1) * HD, :] = (part / total).astype(jnp.bfloat16)


def backward_kernel(
    groups,
    query_ref,
    kv_ref,
    grad_ref,
    attended_ref,
    log_ref,
    gram_ref,
    grad_query_ref,
    grad_kv_ref,
    squares_ref,
    sum_ref,
    row_dot_ref,
):
    rows = query_ref.shape[0]
    blocks = kv_ref.shape[0] // rows
    heads = groups * GROUP
    own = lax.axis_index("ctx")

    def prepare(head, _):
        attended = attended_ref[columns(head), :]
        grad_turned = grad_ref[:, columns(head)].T
        row_dot_ref[pl.ds(head, 1), :] = jnp.sum(
            attended.astype(jnp.float32) * grad_turned.astype(jnp.float32), axis=0, keepdims=True
        )
        attended_rows = attended.T
        products = dot(attended_rows, attended_rows, 1, 1) * gram_ref[rows:, :]
        squares_ref[pl.ds(heads + head, 1), :] = jnp.sum(products, axis=0, keepdims=True)
        return 0

    lax.fori_loop(0, heads, prepare, 0)

    def block(number, diagonal):
        row_at = pl.ds(pl.multiple_of(number * rows, rows), rows)

        def one_group(group, _):
            key_block = kv_ref[row_at, columns(group)]
            value_block = kv_ref[row_at, columns(groups + group)]
            key_turned = key_block.T
            key_sum = jnp.zeros((rows, HD), jnp.float32)
            value_sum = jnp.zeros((rows, HD), jnp.float32)
            for member in range(GROUP):
                head = group * GROUP + member
                one = pl.ds(head, 1)
                query = query_ref[:, columns(head)]
                grad = grad_ref[:, columns(head)]
                scores = dot(key_block, query, 1, 1)
                softmax = jnp.exp2(scores * SCALE2 - log_ref[one, :])
                if diagonal:
                    softmax = jnp.where(causal_keep(rows), softmax, 0.0)
                grad_prob = dot(value_block, grad, 1, 1)
                grad_score = (softmax * (grad_prob - row_dot_ref[one, :])).astype(jnp.bfloat16)
                value_sum = value_sum + dot(softmax.astype(jnp.bfloat16), grad, 1, 0)
                key_sum = key_sum + dot(grad_score, query, 1, 0)
                part = dot(key_turned, grad_score, 1, 0)
                if diagonal:
                    sum_ref[columns(head), :] = part
                else:
                    sum_ref[columns(head), :] += part
            grad_kv_ref[row_at, columns(group)] = (key_sum * SCALING).astype(jnp.bfloat16)
            grad_kv_ref[row_at, columns(groups + group)] = value_sum.astype(jnp.bfloat16)
            return 0

        lax.fori_loop(0, groups, one_group, 0)

    block(own, True)

    def step(number, _):
        block(number, False)
        return 0

    lax.fori_loop(0, own, step, 0)

    def clear(number, _):
        row_at = pl.ds(pl.multiple_of(number * rows, rows), rows)
        grad_kv_ref[row_at, :] = jnp.zeros((rows, 2 * groups * HD), jnp.bfloat16)
        return 0

    lax.fori_loop(own + 1, blocks, clear, 0)

    def finish(head, _):
        grad_query = (sum_ref[columns(head), :] * SCALING).T.astype(jnp.bfloat16)
        grad_query_ref[:, columns(head)] = grad_query
        products = dot(grad_query, grad_query, 1, 1) * gram_ref[:rows, :]
        squares_ref[pl.ds(head, 1), :] = jnp.sum(products, axis=0, keepdims=True)
        return 0

    lax.fori_loop(0, heads, finish, 0)


def whole_vmem(count):
    return [pl.BlockSpec(memory_space=pltpu.VMEM)] * count


def body(model, hidden_in, query_rows, key_rows, value_rows, out_weight, grad_out, answer_mask):
    rows, width = query_rows.shape
    groups = key_rows.shape[1] // HD
    heads = groups * GROUP
    loss_weight = 0.25 + answer_mask.astype(jnp.float32)
    weighted = (grad_out.astype(jnp.float32) * loss_weight[:, None]).astype(jnp.bfloat16)
    kv_all = lax.all_gather(
        jnp.concatenate([key_rows, value_rows], axis=1), "ctx", axis=0, tiled=True
    )
    piece_part = lax.all_gather(weighted, "head", axis=1, tiled=True)
    tokens = kv_all.shape[0]
    grams = jnp.concatenate(
        [dot(hidden_in, hidden_in, 1, 1), dot(weighted, weighted, 1, 1)], axis=0
    )
    grams = lax.psum(grams, "head")
    pairs = rows * tokens * heads * HD * 2
    attended, log_total = pl.pallas_call(
        functools.partial(forward_kernel, groups),
        out_shape=(
            jax.ShapeDtypeStruct((width, rows), jnp.bfloat16),
            jax.ShapeDtypeStruct((heads, rows), jnp.float32),
        ),
        in_specs=whole_vmem(2),
        out_specs=tuple(whole_vmem(2)),
        scratch_shapes=[
            pltpu.VMEM((width, rows), jnp.float32),
            pltpu.VMEM((heads, rows), jnp.float32),
            pltpu.VMEM((heads, rows), jnp.float32),
        ],
        compiler_params=pltpu.CompilerParams(vmem_limit_bytes=VMEM_LIMIT),
        cost_estimate=pl.CostEstimate(
            flops=4 * pairs, bytes_accessed=8 << 20, transcendentals=rows * tokens * heads
        ),
        name="forward",
    )(query_rows, kv_all)
    grad_attended = dot(piece_part, out_weight, 1, 1).astype(jnp.bfloat16)
    grad_query, grad_kv, squares = pl.pallas_call(
        functools.partial(backward_kernel, groups),
        out_shape=(
            jax.ShapeDtypeStruct((rows, width), jnp.bfloat16),
            jax.ShapeDtypeStruct((tokens, 2 * groups * HD), jnp.bfloat16),
            jax.ShapeDtypeStruct((2 * heads, rows), jnp.float32),
        ),
        in_specs=whole_vmem(6),
        out_specs=tuple(whole_vmem(3)),
        scratch_shapes=[
            pltpu.VMEM((width, rows), jnp.float32),
            pltpu.VMEM((heads, rows), jnp.float32),
        ],
        compiler_params=pltpu.CompilerParams(vmem_limit_bytes=VMEM_LIMIT),
        cost_estimate=pl.CostEstimate(
            flops=10 * pairs, bytes_accessed=8 << 20, transcendentals=rows * tokens * heads
        ),
        name="backward",
    )(query_rows, kv_all, grad_attended, attended, log_total, grams)
    key_sums = lax.psum_scatter(grad_kv, "ctx", scatter_dimension=0, tiled=True)
    grad_key = key_sums[:, : groups * HD]
    grad_value = key_sums[:, groups * HD :]
    normal_size = model * HD * rows
    sums = jnp.maximum(jnp.sum(squares, axis=1), 0.0)
    fisher = jnp.log(sums / normal_size + EPSILON).reshape(2, heads)
    return (grad_query, grad_key, grad_value, fisher[:1], fisher[1:])


def solution(mesh):
    spread = P("ctx", "head")

    def whole(hidden_in, *others):
        return jax.shard_map(
            functools.partial(body, hidden_in.shape[1]),
            mesh=mesh,
            in_specs=(spread, spread, spread, spread, P("head", None), spread, P("ctx")),
            out_specs=(spread,) * 5,
            check_vma=False,
        )(hidden_in, *others)

    return whole
```

```python
import functools

import jax
import jax.numpy as jnp
from jax import lax
from jax.experimental import pallas as pl
from jax.experimental.pallas import tpu as pltpu
from jax.sharding import PartitionSpec as P

HD = 128
GROUP = 8
NEGATIVE = -1e30
EPSILON = 1e-06
SCALING = HD ** (-0.5)
LOG2E = 1.4426950408889634
SCALE2 = SCALING * LOG2E
VMEM_LIMIT = 56 * 1024 * 1024


def dot(left, right, left_dim, right_dim):
    return lax.dot_general(
        left, right, (((left_dim,), (right_dim,)), ((), ())), preferred_element_type=jnp.float32
    )


def columns(index):
    if isinstance(index, int):
        return slice(index * HD, (index + 1) * HD)
    return pl.ds(pl.multiple_of(index * HD, HD), HD)


def causal_keep(rows):
    key_pos = lax.broadcasted_iota(jnp.int32, (rows, rows), 0)
    query_pos = lax.broadcasted_iota(jnp.int32, (rows, rows), 1)
    return key_pos <= query_pos


def forward_kernel(groups, query_ref, kv_ref, attended_ref, log_ref, sum_ref, max_ref, total_ref):
    rows = query_ref.shape[0]
    own = lax.axis_index("ctx")

    def block(number, diagonal):
        row_at = pl.ds(pl.multiple_of(number * rows, rows), rows)

        for group in range(groups):
            key_block = kv_ref[row_at, columns(group)]
            value_turned = kv_ref[row_at, columns(groups + group)].T
            for member in range(GROUP):
                head = group * GROUP + member
                scores = dot(key_block, query_ref[:, columns(head)], 1, 1)
                one = slice(head, head + 1)
                if diagonal:
                    scores = jnp.where(causal_keep(rows), scores, NEGATIVE)
                    new_max = jnp.max(scores, axis=0, keepdims=True)
                else:
                    old_max = max_ref[one, :]
                    new_max = jnp.maximum(old_max, jnp.max(scores, axis=0, keepdims=True))
                weights = jnp.exp2(scores * SCALE2 - new_max * SCALE2)
                weights_sum = jnp.sum(weights, axis=0, keepdims=True)
                part = dot(value_turned, weights.astype(jnp.bfloat16), 1, 0)
                if diagonal:
                    total_ref[one, :] = weights_sum
                    sum_ref[columns(head), :] = part
                else:
                    factor = jnp.exp2((old_max - new_max) * SCALE2)
                    total_ref[one, :] = total_ref[one, :] * factor + weights_sum
                    sum_ref[columns(head), :] = sum_ref[columns(head), :] * factor + part
                max_ref[one, :] = new_max

    block(own, True)

    def step(number, _):
        block(number, False)
        return 0

    lax.fori_loop(0, own, step, 0)
    for head in range(groups * GROUP):
        total = total_ref[head : head + 1, :]
        log_ref[head : head + 1, :] = max_ref[head : head + 1, :] * SCALE2 + jnp.log2(total)
        part = sum_ref[head * HD : (head + 1) * HD, :]
        attended_ref[head * HD : (head + 1) * HD, :] = (part / total).astype(jnp.bfloat16)


def backward_kernel(
    groups,
    group,
    query_ref,
    kv_ref,
    grad_ref,
    attended_ref,
    log_ref,
    grad_query_ref,
    grad_kv_ref,
    sum_ref,
    row_dot_ref,
):
    rows = query_ref.shape[0]
    blocks = kv_ref.shape[0] // rows
    own = lax.axis_index("ctx")
    for member in range(GROUP):
        head = group * GROUP + member
        attended = attended_ref[columns(head), :]
        grad_turned = grad_ref[:, columns(head)].T
        row_dot_ref[member : member + 1, :] = jnp.sum(
            attended.astype(jnp.float32) * grad_turned.astype(jnp.float32), axis=0, keepdims=True
        )

    def block(number, diagonal):
        row_at = pl.ds(pl.multiple_of(number * rows, rows), rows)

        key_block = kv_ref[row_at, columns(group)]
        value_block = kv_ref[row_at, columns(groups + group)]
        key_turned = key_block.T
        key_sum = jnp.zeros((rows, HD), jnp.float32)
        value_sum = jnp.zeros((rows, HD), jnp.float32)
        for member in range(GROUP):
            head = group * GROUP + member
            query = query_ref[:, columns(head)]
            grad = grad_ref[:, columns(head)]
            scores = dot(key_block, query, 1, 1)
            softmax = jnp.exp2(scores * SCALE2 - log_ref[head : head + 1, :])
            if diagonal:
                softmax = jnp.where(causal_keep(rows), softmax, 0.0)
            grad_prob = dot(value_block, grad, 1, 1)
            row_dot = row_dot_ref[member : member + 1, :]
            grad_score = (softmax * (grad_prob - row_dot)).astype(jnp.bfloat16)
            value_sum = value_sum + dot(softmax.astype(jnp.bfloat16), grad, 1, 0)
            key_sum = key_sum + dot(grad_score, query, 1, 0)
            part = dot(key_turned, grad_score, 1, 0)
            if diagonal:
                sum_ref[columns(member), :] = part
            else:
                sum_ref[columns(member), :] += part
        grad_kv_ref[row_at, :HD] = (key_sum * SCALING).astype(jnp.bfloat16)
        grad_kv_ref[row_at, HD:] = value_sum.astype(jnp.bfloat16)

    block(own, True)

    def step(number, _):
        block(number, False)
        return 0

    lax.fori_loop(0, own, step, 0)

    def clear(number, _):
        row_at = pl.ds(pl.multiple_of(number * rows, rows), rows)
        grad_kv_ref[row_at, :] = jnp.zeros((rows, 2 * HD), jnp.bfloat16)
        return 0

    lax.fori_loop(own + 1, blocks, clear, 0)

    for member in range(GROUP):
        grad_query = (sum_ref[columns(member), :] * SCALING).T.astype(jnp.bfloat16)
        grad_query_ref[:, columns(member)] = grad_query


def squares_kernel(heads, grad_query_ref, attended_ref, gram_ref, squares_ref):
    rows = grad_query_ref.shape[0]

    def one_head(head, _):
        grad_query = grad_query_ref[:, columns(head)]
        products = dot(grad_query, grad_query, 1, 1) * gram_ref[:rows, :]
        squares_ref[pl.ds(head, 1), :] = jnp.sum(products, axis=0, keepdims=True)
        attended = attended_ref[columns(head), :].T
        products = dot(attended, attended, 1, 1) * gram_ref[rows:, :]
        squares_ref[pl.ds(heads + head, 1), :] = jnp.sum(products, axis=0, keepdims=True)
        return 0

    lax.fori_loop(0, heads, one_head, 0)


def whole_vmem(count):
    return [pl.BlockSpec(memory_space=pltpu.VMEM)] * count


def body(model, hidden_in, query_rows, key_rows, value_rows, out_weight, grad_out, answer_mask):
    rows, width = query_rows.shape
    groups = key_rows.shape[1] // HD
    heads = groups * GROUP
    loss_weight = 0.25 + answer_mask.astype(jnp.float32)
    weighted = (grad_out.astype(jnp.float32) * loss_weight[:, None]).astype(jnp.bfloat16)
    kv_all = lax.all_gather(
        jnp.concatenate([key_rows, value_rows], axis=1), "ctx", axis=0, tiled=True
    )
    own_head = lax.axis_index("head")
    head_devices = model // width
    piece_part = jnp.zeros((rows, model), jnp.bfloat16)
    pieces = [weighted] + [
        lax.ppermute(weighted, "head", [(at, at ^ far) for at in range(head_devices)])
        for far in range(1, head_devices)
    ]
    tokens = kv_all.shape[0]
    grams = jnp.concatenate(
        [dot(hidden_in, hidden_in, 1, 1), dot(weighted, weighted, 1, 1)], axis=0
    )
    pairs = rows * tokens * heads * HD * 2
    attended, log_total = pl.pallas_call(
        functools.partial(forward_kernel, groups),
        out_shape=(
            jax.ShapeDtypeStruct((width, rows), jnp.bfloat16),
            jax.ShapeDtypeStruct((heads, rows), jnp.float32),
        ),
        in_specs=whole_vmem(2),
        out_specs=tuple(whole_vmem(2)),
        scratch_shapes=[
            pltpu.VMEM((width, rows), jnp.float32),
            pltpu.VMEM((heads, rows), jnp.float32),
            pltpu.VMEM((heads, rows), jnp.float32),
        ],
        compiler_params=pltpu.CompilerParams(vmem_limit_bytes=VMEM_LIMIT),
        cost_estimate=pl.CostEstimate(
            flops=4 * pairs, bytes_accessed=8 << 20, transcendentals=rows * tokens * heads
        ),
        name="forward",
    )(query_rows, kv_all)
    grams, attended = lax.optimization_barrier((grams, attended))
    grams = lax.psum(grams, "head")
    attended, *pieces = lax.optimization_barrier((attended, *pieces))
    for far, piece in enumerate(pieces):
        piece_part = lax.dynamic_update_slice(piece_part, piece, (0, (own_head ^ far) * width))
    grad_attended = dot(piece_part, out_weight, 1, 1).astype(jnp.bfloat16)
    query_grads, key_grads, value_grads = [], [], []
    for group in range(groups):
        grad_part, grad_kv = pl.pallas_call(
            functools.partial(backward_kernel, groups, group),
            out_shape=(
                jax.ShapeDtypeStruct((rows, GROUP * HD), jnp.bfloat16),
                jax.ShapeDtypeStruct((tokens, 2 * HD), jnp.bfloat16),
            ),
            in_specs=whole_vmem(5),
            out_specs=tuple(whole_vmem(2)),
            scratch_shapes=[
                pltpu.VMEM((GROUP * HD, rows), jnp.float32),
                pltpu.VMEM((GROUP, rows), jnp.float32),
            ],
            compiler_params=pltpu.CompilerParams(vmem_limit_bytes=VMEM_LIMIT),
            cost_estimate=pl.CostEstimate(
                flops=10 * pairs // groups,
                bytes_accessed=8 << 20,
                transcendentals=rows * tokens * GROUP,
            ),
            name="backward",
        )(query_rows, kv_all, grad_attended, attended, log_total)
        key_sums = lax.psum_scatter(grad_kv, "ctx", scatter_dimension=0, tiled=True)
        query_grads.append(grad_part)
        key_grads.append(key_sums[:, :HD])
        value_grads.append(key_sums[:, HD:])
    grad_query = jnp.concatenate(query_grads, axis=1)
    grad_key = jnp.concatenate(key_grads, axis=1)
    grad_value = jnp.concatenate(value_grads, axis=1)
    squares = pl.pallas_call(
        functools.partial(squares_kernel, heads),
        out_shape=jax.ShapeDtypeStruct((2 * heads, rows), jnp.float32),
        in_specs=whole_vmem(3),
        out_specs=whole_vmem(1)[0],
        compiler_params=pltpu.CompilerParams(vmem_limit_bytes=VMEM_LIMIT),
        name="squares",
    )(grad_query, attended, grams)
    normal_size = model * HD * rows
    sums = jnp.maximum(jnp.sum(squares, axis=1), 0.0)
    fisher = jnp.log(sums / normal_size + EPSILON).reshape(2, heads)
    return (grad_query, grad_key, grad_value, fisher[:1], fisher[1:])


def solution(mesh):
    spread = P("ctx", "head")

    def whole(hidden_in, *others):
        return jax.shard_map(
            functools.partial(body, hidden_in.shape[1]),
            mesh=mesh,
            in_specs=(spread, spread, spread, spread, P("head", None), spread, P("ctx")),
            out_specs=(spread,) * 5,
            check_vma=False,
        )(hidden_in, *others)

    return whole
```

```python
import functools

import jax
import jax.numpy as jnp
from jax import lax
from jax.experimental import pallas as pl
from jax.experimental.pallas import tpu as pltpu
from jax.sharding import PartitionSpec as P

HD = 128
GROUP = 8
NEGATIVE = -1e30
EPSILON = 1e-06
SCALING = HD ** (-0.5)
LOG2E = 1.4426950408889634
SCALE2 = SCALING * LOG2E
VMEM_LIMIT = 56 * 1024 * 1024


def dot(left, right, left_dim, right_dim):
    return lax.dot_general(
        left, right, (((left_dim,), (right_dim,)), ((), ())), preferred_element_type=jnp.float32
    )


def columns(index):
    if isinstance(index, int):
        return slice(index * HD, (index + 1) * HD)
    return pl.ds(pl.multiple_of(index * HD, HD), HD)


def causal_keep(rows):
    key_pos = lax.broadcasted_iota(jnp.int32, (rows, rows), 0)
    query_pos = lax.broadcasted_iota(jnp.int32, (rows, rows), 1)
    return key_pos <= query_pos


def forward_kernel(groups, query_ref, kv_ref, attended_ref, log_ref, sum_ref, max_ref, total_ref):
    rows = query_ref.shape[0]
    own = lax.axis_index("ctx")

    def block(number, diagonal):
        row_at = pl.ds(pl.multiple_of(number * rows, rows), rows)

        for group in range(groups):
            key_block = kv_ref[row_at, columns(group)]
            value_turned = kv_ref[row_at, columns(groups + group)].T
            for member in range(GROUP):
                head = group * GROUP + member
                scores = dot(key_block, query_ref[:, columns(head)], 1, 1)
                one = slice(head, head + 1)
                if diagonal:
                    scores = jnp.where(causal_keep(rows), scores, NEGATIVE)
                    new_max = jnp.max(scores, axis=0, keepdims=True)
                else:
                    old_max = max_ref[one, :]
                    new_max = jnp.maximum(old_max, jnp.max(scores, axis=0, keepdims=True))
                weights = jnp.exp2(scores * SCALE2 - new_max * SCALE2)
                weights_sum = jnp.sum(weights, axis=0, keepdims=True)
                part = dot(value_turned, weights.astype(jnp.bfloat16), 1, 0)
                if diagonal:
                    total_ref[one, :] = weights_sum
                    sum_ref[columns(head), :] = part
                else:
                    factor = jnp.exp2((old_max - new_max) * SCALE2)
                    total_ref[one, :] = total_ref[one, :] * factor + weights_sum
                    sum_ref[columns(head), :] = sum_ref[columns(head), :] * factor + part
                max_ref[one, :] = new_max

    block(own, True)

    def step(number, _):
        block(number, False)
        return 0

    lax.fori_loop(0, own, step, 0)
    for head in range(groups * GROUP):
        total = total_ref[head : head + 1, :]
        log_ref[head : head + 1, :] = max_ref[head : head + 1, :] * SCALE2 + jnp.log2(total)
        part = sum_ref[head * HD : (head + 1) * HD, :]
        attended_ref[head * HD : (head + 1) * HD, :] = (part / total).astype(jnp.bfloat16)


def backward_kernel(
    groups,
    group,
    query_ref,
    kv_ref,
    grad_ref,
    attended_ref,
    log_ref,
    grad_query_ref,
    grad_kv_ref,
    sum_ref,
    row_dot_ref,
):
    rows = query_ref.shape[0]
    blocks = kv_ref.shape[0] // rows
    own = lax.axis_index("ctx")
    for member in range(GROUP):
        head = group * GROUP + member
        attended = attended_ref[columns(head), :]
        grad_turned = grad_ref[:, columns(head)].T
        row_dot_ref[member : member + 1, :] = jnp.sum(
            attended.astype(jnp.float32) * grad_turned.astype(jnp.float32), axis=0, keepdims=True
        )

    def block(number, diagonal):
        row_at = pl.ds(pl.multiple_of(number * rows, rows), rows)

        key_block = kv_ref[row_at, columns(group)]
        value_block = kv_ref[row_at, columns(groups + group)]
        key_turned = key_block.T
        key_sum = jnp.zeros((rows, HD), jnp.float32)
        value_sum = jnp.zeros((rows, HD), jnp.float32)
        for member in range(GROUP):
            head = group * GROUP + member
            query = query_ref[:, columns(head)]
            grad = grad_ref[:, columns(head)]
            scores = dot(key_block, query, 1, 1)
            softmax = jnp.exp2(scores * SCALE2 - log_ref[head : head + 1, :])
            if diagonal:
                softmax = jnp.where(causal_keep(rows), softmax, 0.0)
            grad_prob = dot(value_block, grad, 1, 1)
            row_dot = row_dot_ref[member : member + 1, :]
            grad_score = (softmax * (grad_prob - row_dot)).astype(jnp.bfloat16)
            value_sum = value_sum + dot(softmax.astype(jnp.bfloat16), grad, 1, 0)
            key_sum = key_sum + dot(grad_score, query, 1, 0)
            part = dot(key_turned, grad_score, 1, 0)
            if diagonal:
                sum_ref[columns(member), :] = part
            else:
                sum_ref[columns(member), :] += part
        grad_kv_ref[row_at, :HD] = (key_sum * SCALING).astype(jnp.bfloat16)
        grad_kv_ref[row_at, HD:] = value_sum.astype(jnp.bfloat16)

    block(own, True)

    def step(number, _):
        block(number, False)
        return 0

    lax.fori_loop(0, own, step, 0)

    def clear(number, _):
        row_at = pl.ds(pl.multiple_of(number * rows, rows), rows)
        grad_kv_ref[row_at, :] = jnp.zeros((rows, 2 * HD), jnp.bfloat16)
        return 0

    lax.fori_loop(own + 1, blocks, clear, 0)

    for member in range(GROUP):
        grad_query = (sum_ref[columns(member), :] * SCALING).T.astype(jnp.bfloat16)
        grad_query_ref[:, columns(member)] = grad_query


def squares_kernel(heads, grad_query_ref, attended_ref, gram_ref, squares_ref):
    rows = grad_query_ref.shape[0]

    def one_head(head, _):
        grad_query = grad_query_ref[:, columns(head)]
        products = dot(grad_query, grad_query, 1, 1) * gram_ref[:rows, :]
        squares_ref[pl.ds(head, 1), :] = jnp.sum(products, axis=0, keepdims=True)
        attended = attended_ref[columns(head), :].T
        products = dot(attended, attended, 1, 1) * gram_ref[rows:, :]
        squares_ref[pl.ds(heads + head, 1), :] = jnp.sum(products, axis=0, keepdims=True)
        return 0

    lax.fori_loop(0, heads, one_head, 0)


def whole_vmem(count):
    return [pl.BlockSpec(memory_space=pltpu.VMEM)] * count


def project_kernel(own_ref, *refs):
    *piece_refs, weight_ref, out_ref, sum_ref = refs
    far = pl.program_id(0)
    tile = weight_ref.shape[0]
    at = pl.ds(pl.multiple_of(pl.program_id(1) * tile, tile), tile)
    for number, piece_ref in enumerate(piece_refs):

        @pl.when(far == number)
        def _():
            total = dot(piece_ref[...], weight_ref[...], 1, 1)
            if number:
                total = total + sum_ref[:, at]
            if number < len(piece_refs) - 1:
                sum_ref[:, at] = total
            else:
                out_ref[:, at] = total.astype(jnp.bfloat16)


def project(own_head, pieces, out_weight):
    rows, width = pieces[0].shape
    outs = out_weight.shape[0]
    tile = 512
    whole = pl.BlockSpec((rows, width), lambda far, at, own: (0, 0))
    return pl.pallas_call(
        project_kernel,
        out_shape=jax.ShapeDtypeStruct((rows, outs), jnp.bfloat16),
        grid_spec=pltpu.PrefetchScalarGridSpec(
            num_scalar_prefetch=1,
            grid=(len(pieces), outs // tile),
            in_specs=[whole] * len(pieces)
            + [pl.BlockSpec((tile, width), lambda far, at, own: (at, own[0] ^ far))],
            out_specs=pl.BlockSpec((rows, outs), lambda far, at, own: (0, 0)),
            scratch_shapes=[pltpu.VMEM((rows, outs), jnp.float32)],
        ),
        compiler_params=pltpu.CompilerParams(vmem_limit_bytes=VMEM_LIMIT),
        name="project",
    )(jnp.reshape(own_head, (1,)).astype(jnp.int32), *pieces, out_weight)


def owner_sums(parts, rows):
    count = parts.shape[0] // rows
    own = lax.axis_index("ctx")
    core, chip = own % 2, own // 2
    blocks = parts.reshape(count // 2, 2, rows, parts.shape[1])

    def of_core(index):
        return lax.dynamic_index_in_dim(blocks, index, 1, keepdims=False)

    def swapped(value, far):
        return lax.ppermute(value, "ctx", [(at, at ^ far) for at in range(count)])

    got = swapped(of_core(1 - core), 1)
    pair = of_core(core).astype(jnp.float32) + got.astype(jnp.float32)
    pair = pair.astype(jnp.bfloat16)
    total = lax.dynamic_index_in_dim(pair, chip, 0, keepdims=False).astype(jnp.float32)
    for far in range(1, count // 2):
        piece = lax.dynamic_index_in_dim(pair, chip ^ far, 0, keepdims=False)
        total = total + swapped(piece, 2 * far).astype(jnp.float32)
    return total.astype(jnp.bfloat16)


def body(model, hidden_in, query_rows, key_rows, value_rows, out_weight, grad_out, answer_mask):
    rows, width = query_rows.shape
    groups = key_rows.shape[1] // HD
    heads = groups * GROUP
    loss_weight = 0.25 + answer_mask.astype(jnp.float32)
    weighted = (grad_out.astype(jnp.float32) * loss_weight[:, None]).astype(jnp.bfloat16)
    kv_all = lax.all_gather(
        jnp.concatenate([key_rows, value_rows], axis=1), "ctx", axis=0, tiled=True
    )
    own_head = lax.axis_index("head")
    head_devices = model // width
    pieces = [weighted] + [
        lax.ppermute(weighted, "head", [(at, at ^ far) for at in range(head_devices)])
        for far in range(1, head_devices)
    ]
    tokens = kv_all.shape[0]
    grams = jnp.concatenate(
        [dot(hidden_in, hidden_in, 1, 1), dot(weighted, weighted, 1, 1)], axis=0
    )
    pairs = rows * tokens * heads * HD * 2
    attended, log_total = pl.pallas_call(
        functools.partial(forward_kernel, groups),
        out_shape=(
            jax.ShapeDtypeStruct((width, rows), jnp.bfloat16),
            jax.ShapeDtypeStruct((heads, rows), jnp.float32),
        ),
        in_specs=whole_vmem(2),
        out_specs=tuple(whole_vmem(2)),
        scratch_shapes=[
            pltpu.VMEM((width, rows), jnp.float32),
            pltpu.VMEM((heads, rows), jnp.float32),
            pltpu.VMEM((heads, rows), jnp.float32),
        ],
        compiler_params=pltpu.CompilerParams(vmem_limit_bytes=VMEM_LIMIT),
        cost_estimate=pl.CostEstimate(
            flops=4 * pairs, bytes_accessed=8 << 20, transcendentals=rows * tokens * heads
        ),
        name="forward",
    )(query_rows, kv_all)
    grams, attended = lax.optimization_barrier((grams, attended))
    grams = lax.psum(grams, "head")
    attended, *pieces = lax.optimization_barrier((attended, *pieces))
    grad_attended = project(own_head, pieces, out_weight)
    query_grads, key_grads, value_grads = [], [], []
    for group in range(groups):
        grad_part, grad_kv = pl.pallas_call(
            functools.partial(backward_kernel, groups, group),
            out_shape=(
                jax.ShapeDtypeStruct((rows, GROUP * HD), jnp.bfloat16),
                jax.ShapeDtypeStruct((tokens, 2 * HD), jnp.bfloat16),
            ),
            in_specs=whole_vmem(5),
            out_specs=tuple(whole_vmem(2)),
            scratch_shapes=[
                pltpu.VMEM((GROUP * HD, rows), jnp.float32),
                pltpu.VMEM((GROUP, rows), jnp.float32),
            ],
            compiler_params=pltpu.CompilerParams(vmem_limit_bytes=VMEM_LIMIT),
            cost_estimate=pl.CostEstimate(
                flops=10 * pairs // groups,
                bytes_accessed=8 << 20,
                transcendentals=rows * tokens * GROUP,
            ),
            name="backward",
        )(query_rows, kv_all, grad_attended, attended, log_total)
        key_sums = owner_sums(grad_kv, rows)
        query_grads.append(grad_part)
        key_grads.append(key_sums[:, :HD])
        value_grads.append(key_sums[:, HD:])
    grad_query = jnp.concatenate(query_grads, axis=1)
    grad_key = jnp.concatenate(key_grads, axis=1)
    grad_value = jnp.concatenate(value_grads, axis=1)
    squares = pl.pallas_call(
        functools.partial(squares_kernel, heads),
        out_shape=jax.ShapeDtypeStruct((2 * heads, rows), jnp.float32),
        in_specs=whole_vmem(3),
        out_specs=whole_vmem(1)[0],
        compiler_params=pltpu.CompilerParams(vmem_limit_bytes=VMEM_LIMIT),
        name="squares",
    )(grad_query, attended, grams)
    normal_size = model * HD * rows
    sums = jnp.maximum(jnp.sum(squares, axis=1), 0.0)
    fisher = jnp.log(sums / normal_size + EPSILON).reshape(2, heads)
    return (grad_query, grad_key, grad_value, fisher[:1], fisher[1:])


def solution(mesh):
    spread = P("ctx", "head")

    def whole(hidden_in, *others):
        return jax.shard_map(
            functools.partial(body, hidden_in.shape[1]),
            mesh=mesh,
            in_specs=(spread, spread, spread, spread, P("head", None), spread, P("ctx")),
            out_specs=(spread,) * 5,
            check_vma=False,
        )(hidden_in, *others)

    return whole
```
